32 devices in a mesh: dp: 32 (over z, y, x, core).
Axes of the slice: x: 2, y: 2, z: 4, core: 2. Of those that a mesh axis runs over, the one named last changes fastest.
Arguments:
- inputs: bfloat16 [32768, 1024], P('dp'), may hold values from -6 to 6
- seq_lengths: int32 [64, 4], P('dp'), may hold values from 1 to 256, 512 in all within a row
- qkv_weight: bfloat16 [1024, 3072], P('dp'), may hold values from -0.1875 to 0.1875
- out_weight: bfloat16 [1024, 1024], P('dp'), may hold values from -0.75 to 0.75
- up_weight: bfloat16 [1024, 4096], P('dp'), may hold values from -0.1875 to 0.1875
- down_weight: bfloat16 [4096, 1024], P('dp'), may hold values from -0.09375 to 0.09375
- query_bias: bfloat16 [1024], P('dp'), may hold values from -3 to 3
- value_bias: bfloat16 [1024], P('dp'), may hold values from -3 to 3
- out_bias: bfloat16 [1024], P('dp'), may hold values from -3 to 3
- up_bias: bfloat16 [4096], P('dp'), may hold values from -3 to 3
- down_bias: bfloat16 [1024], P('dp'), may hold values from -3 to 3
- first_gain: bfloat16 [1024], P('dp'), may hold values from 0.5 to 1.5
- first_shift: bfloat16 [1024], P('dp'), may hold values from -3 to 3
- second_gain: bfloat16 [1024], P('dp'), may hold values from 0.5 to 1.5
- second_shift: bfloat16 [1024], P('dp'), may hold values from -3 to 3
- grad_output: bfloat16 [32768, 1024], P('dp'), may hold values from -6 to 6
Outputs:
- output: bfloat16 [32768, 1024], P('dp')
- grad_inputs: bfloat16 [32768, 1024], P('dp')
- grad_qkv: float32 [1024, 3072], P('dp')
- grad_out: float32 [1024, 1024], P('dp')
- grad_up: float32 [1024, 4096], P('dp')
- grad_down: float32 [4096, 1024], P('dp')
- grad_query_bias: float32 [1024], P('dp')
- grad_value_bias: float32 [1024], P('dp')
- grad_out_bias: float32 [1024], P('dp')
- grad_up_bias: float32 [4096], P('dp')
- grad_down_bias: float32 [1024], P('dp')
- grad_first_gain: float32 [1024], P('dp')
- grad_first_shift: float32 [1024], P('dp')
- grad_second_gain: float32 [1024], P('dp')
- grad_second_shift: float32 [1024], P('dp')
The draws below stay inside these ranges and needn't reach their ends.
Inputs may be any that keep to these rules, and one draw needn't show every extreme that they name: `seq_lengths`: each row lists the lengths of the 4 sequences packed in order into one block of 512 tokens; every row sums to 512 and its largest entry is exactly 256. Device d holds rows d * 2 to d * 2 + 1, one per micro-batch.
All inputs are finite; a program needn't handle non-finite values.
Results may differ from the reference program's by a relative error of at most 0.013.
Values may be sent and summed in bfloat16 or wider, within the bound.
A program may use at most 256 MiB of HBM per device.

```python
import math
import jax
import jax.numpy as jnp
import numpy as np
from jax import lax

D = 1024
FF = 4096
HEADS = 16
SEQS = 4
SLOT = 512
SLOTS = 64
TOKENS = 32768


def spiked(array, key, source, target, parts, factor):
    owner, partner = [(jnp.arange(array.shape[axis_at]) // (array.shape[axis_at] // parts)).reshape([-1 if axis == axis_at else 1 for axis in range(array.ndim)]) for axis_at in (source, target)]
    chosen = jax.random.permutation(key, parts)[partner]
    strong = (owner == chosen) | (owner == (partner + parts // 2) % parts)
    return jnp.where(strong, factor * array, array)


def shard_levels(key, extent, cuts, low, largest):
    loudness = 1.0
    for axis_at, parts in cuts:
        draws = jax.random.uniform(jax.random.fold_in(jax.random.fold_in(key, 6), axis_at), (parts,), jnp.float32, low / len(cuts), largest / len(cuts))
        loudness = loudness * jnp.repeat(jnp.exp(draws), extent[axis_at] // parts).reshape((-1,) + (1,) * (len(extent) - 1 - axis_at))
    return loudness


def profile(count, total, bound, skew):
    weights = [(1 << 20) // math.isqrt(rank ** skew) + 1 for rank in range(2, count + 1)]
    spare, given = total - bound - (count - 1), [1] * (count - 1)
    while spare > 0:
        movable = [i for i in range(count - 1) if given[i] < bound]
        mass, left = sum([weights[i] for i in movable]), spare
        for i in movable:
            more = min(bound - given[i], max(1, left * weights[i] // mass), spare)
            given[i] = given[i] + more
            spare = spare - more
    return np.array([bound] + given)


def ragged_sizes(stream_key, number_of, total, bound, slope):
    if number_of == 2:
        one = jax.random.randint(stream_key, (), max(1, total - bound), min(bound, total - 1) + 1)
        return jnp.stack([one, total - one])
    tallies = jnp.asarray(profile(number_of, total, bound, slope), jnp.int32)
    pairs = (number_of - 1) // 2
    donor, receiver = tallies[1:1 + 2 * pairs:2], tallies[2:2 + 2 * pairs:2]
    margin = jnp.minimum(donor - 1, bound - receiver)
    shifted = jax.random.randint(jax.random.fold_in(stream_key, 1), (pairs,), 0, 1 << 20) % (margin + 1)
    tallies = tallies.at[1:1 + 2 * pairs:2].set(donor - shifted).at[2:2 + 2 * pairs:2].set(receiver + shifted)
    return tallies[jax.random.permutation(jax.random.fold_in(stream_key, 2), number_of)]


def scatter_about(own_key, dims, spread, reach, cuts=(), kind=jnp.bfloat16):
    values = spread * jax.random.normal(own_key, dims, jnp.float32)
    if cuts:
        values = values * shard_levels(own_key, dims, cuts, -0.22, 0.18)
    return jnp.clip(values, -reach, reach).astype(kind)


def noise_with(own_key, dims, scale, reach, pieces, heavy, held_as=jnp.bfloat16):
    array = scale * jax.random.normal(own_key, dims, jnp.float32)
    if pieces:
        array = array * shard_levels(own_key, dims, pieces, -0.22, 0.18)
    return jnp.clip(spiked(array, jax.random.fold_in(own_key, 3), *heavy), -reach, reach).astype(held_as)


def setup_inputs(seed: int = 0) -> dict:
    key_of = jax.random.split(jax.random.key(seed), 17)
    inputs = scatter_about(key_of[0], (TOKENS, D), 1.0, 6.0, ((0, 32),))
    seq_lengths = jax.vmap(lambda own: ragged_sizes(own, SEQS, SLOT, SLOT // 2, 2))(jax.random.split(key_of[1], SLOTS)).reshape((SLOTS, SEQS)).astype(jnp.int32)
    qkv_weight = scatter_about(key_of[2], (D, 3 * D), D ** -0.5, 0.1875, ((0, 32),))
    out_weight = scatter_about(key_of[3], (D, D), (D // 16) ** -0.5, 0.75, ((0, 32),))
    up_weight = scatter_about(key_of[4], (D, FF), D ** -0.5, 0.1875, ((0, 32),))
    down_weight = scatter_about(key_of[5], (FF, D), FF ** -0.5, 0.09375, ((0, 32),))
    query_bias = scatter_about(key_of[6], (D,), 0.5, 3.0, ((0, 32),))
    value_bias = scatter_about(key_of[7], (D,), 0.5, 3.0, ((0, 32),))
    out_bias = scatter_about(key_of[8], (D,), 0.5, 3.0, ((0, 32),))
    up_bias = scatter_about(key_of[9], (FF,), 0.5, 3.0, ((0, 32),))
    down_bias = scatter_about(key_of[10], (D,), 0.5, 3.0, ((0, 32),))
    first_gain = jnp.clip(1.0 + 0.1 * jax.random.normal(key_of[11], (D,), jnp.float32), 0.5, 1.5).astype(jnp.bfloat16)
    first_shift = scatter_about(key_of[12], (D,), 0.5, 3.0, ((0, 32),))
    second_gain = jnp.clip(1.0 + 0.1 * jax.random.normal(key_of[13], (D,), jnp.float32), 0.5, 1.5).astype(jnp.bfloat16)
    second_shift = scatter_about(key_of[14], (D,), 0.5, 3.0, ((0, 32),))
    grad_output = noise_with(key_of[15], (TOKENS, D), 1.0, 6.0, ((0, 32),), (0, 1, 32, 2.75))
    return dict(inputs=inputs, seq_lengths=seq_lengths, qkv_weight=qkv_weight, out_weight=out_weight, up_weight=up_weight, down_weight=down_weight, query_bias=query_bias, value_bias=value_bias, out_bias=out_bias, up_bias=up_bias, down_bias=down_bias, first_gain=first_gain, first_shift=first_shift, second_gain=second_gain, second_shift=second_shift, grad_output=grad_output)


@jax.custom_vjp
def low(v):
    return lax.optimization_barrier(v.astype(jnp.bfloat16)).astype(jnp.float32)

@jax.custom_vjp
def low_back(v):
    return v

def low_keep(v):
    return (low(v), None)

def low_pass(kept, grad):
    return (grad,)

def back_keep(v):
    return (v, None)

def back_low(kept, grad):
    return (low(grad),)
low.defvjp(low_keep, low_pass)
low_back.defvjp(back_keep, back_low)
epsilon = 1e-05
exact = lax.Precision.HIGHEST

def norm_rows(values, norm_gain, norm_shift):
    center = values - lax.optimization_barrier(jnp.mean(values, axis=-1, keepdims=True))
    variance = lax.optimization_barrier(jnp.mean(center * center, axis=-1, keepdims=True))
    return center * lax.rsqrt(variance + epsilon) * norm_gain + norm_shift

def allowed_pairs(lengths_row, row_count):
    seq_ends = jnp.cumsum(lengths_row).astype(jnp.int32)
    places = jnp.arange(row_count, dtype=jnp.int32)
    labels = lax.optimization_barrier(jnp.sum((places[:, None] >= seq_ends[None, :]).astype(jnp.int32), axis=1)).astype(jnp.int32)
    return labels[:, None] == labels[None, :]

def slot_layer(weights, tokens, lengths_row):
    whole_qkv, whole_out, whole_up, whole_down, bias_query, bias_value, bias_out, bias_up, bias_down, gain_first, shift_first, gain_second, shift_second = weights
    row_count = tokens.shape[0]
    width = tokens.shape[1]
    head_size = width // HEADS
    bias_all = jnp.concatenate([bias_query, jnp.zeros_like(bias_query), bias_value])
    mixed = jnp.dot(tokens, whole_qkv, precision=exact) + bias_all
    mixed = low_back(low(mixed))
    split = mixed.reshape(row_count, 3, HEADS, head_size)
    queries = split[:, 0]
    keys_all = split[:, 1]
    values = split[:, 2]
    raw_scores = jnp.einsum('qhd,khd->hqk', queries, keys_all, precision=exact) * head_size ** (-0.5)
    scores = low_back(raw_scores)
    allowed = allowed_pairs(lengths_row, row_count)
    scores = jnp.where(allowed[None], scores, -1e+30)
    top_score = lax.optimization_barrier(jnp.max(scores, axis=-1, keepdims=True))
    expo = jnp.exp(scores - top_score)
    probs = expo / lax.optimization_barrier(jnp.sum(expo, axis=-1, keepdims=True))
    attended = jnp.einsum('hqk,khd->qhd', low(probs), values, precision=exact).reshape(row_count, width)
    attended = low_back(low(attended))
    branch = low_back(jnp.dot(attended, whole_out, precision=exact) + bias_out)
    hidden = norm_rows(tokens + branch, gain_first, shift_first)
    pre_act = low_back(jnp.dot(low(hidden), whole_up, precision=exact) + bias_up)
    activ = low(jax.nn.gelu(pre_act, approximate=False))
    second = low_back(jnp.dot(activ, whole_down, precision=exact) + bias_down)
    return norm_rows(hidden + second, gain_second, shift_second)

def reference(inputs, seq_lengths, qkv_weight, out_weight, up_weight, down_weight, query_bias, value_bias, out_bias, up_bias, down_bias, first_gain, first_shift, second_gain, second_shift, grad_output):
    weights = tuple((member.astype(jnp.float32) for member in (qkv_weight, out_weight, up_weight, down_weight, query_bias, value_bias, out_bias, up_bias, down_bias, first_gain, first_shift, second_gain, second_shift)))
    tokens = inputs.astype(jnp.float32).reshape(SLOTS, SLOT, D)
    layer = jax.checkpoint(slot_layer)

    def forward(weights_all, tokens_all):

        def one_block(operands):
            return layer(weights_all, operands[0], operands[1])
        return lax.map(one_block, (tokens_all, seq_lengths))
    result, pullback = jax.vjp(forward, weights, tokens)
    grad_weights, grad_tokens = pullback(grad_output.astype(jnp.float32).reshape(SLOTS, SLOT, D))
    return (result.reshape(TOKENS, D).astype(jnp.bfloat16), grad_tokens.reshape(TOKENS, D).astype(jnp.bfloat16), grad_weights[0], grad_weights[1], grad_weights[2], grad_weights[3], grad_weights[4], grad_weights[5], grad_weights[6], grad_weights[7], grad_weights[8], grad_weights[9], grad_weights[10], grad_weights[11], grad_weights[12])
```

```python
import functools
import math

import jax
import jax.numpy as jnp
from jax import lax
from jax.experimental import pallas as pl
from jax.experimental.pallas import tpu as pltpu
from jax.sharding import PartitionSpec as P

HEADS = 16
HEAD_SIZE = 64
LANES = 128
epsilon = 1e-05
VMEM_BYTES = 48 * 1024 * 1024
F32 = jnp.float32
BF16 = jnp.bfloat16


def dot(left, right, left_dim, right_dim):
    return lax.dot_general(
        left, right, (((left_dim,), (right_dim,)), ((), ())), preferred_element_type=F32
    )


def norm_rows(values, norm_gain, norm_shift):
    center = values - jnp.mean(values, axis=-1, keepdims=True)
    variance = jnp.mean(center * center, axis=-1, keepdims=True)
    inverse = lax.rsqrt(variance + epsilon)
    scaled = center * inverse
    return (scaled * norm_gain + norm_shift, scaled, inverse)


def norm_back(gradient, scaled, inverse, norm_gain):
    weighted = gradient * norm_gain
    mean_grad = jnp.mean(weighted, axis=-1, keepdims=True)
    mean_prod = jnp.mean(weighted * scaled, axis=-1, keepdims=True)
    result = inverse * (weighted - mean_grad - scaled * mean_prod)
    return (result, jnp.sum(gradient * scaled, axis=0), jnp.sum(gradient, axis=0))


def head_probs(query, key, allowed):
    scores = jnp.where(allowed, dot(query, key, 1, 1), -1e30)
    expo = jnp.exp(scores - jnp.max(scores, axis=-1, keepdims=True))
    return expo * (1.0 / jnp.sum(expo, axis=-1, keepdims=True))


def attend_kernel(column_ref, row_ref, query_ref, key_ref, value_ref, out_ref):
    allowed = column_ref[...] == row_ref[...]
    for start in range(0, LANES, HEAD_SIZE):
        part = slice(start, start + HEAD_SIZE)
        query = query_ref[:, part] * jnp.asarray(HEAD_SIZE**-0.5, BF16)
        probs = head_probs(query, key_ref[:, part], allowed)
        out_ref[:, part] = dot(probs.astype(BF16), value_ref[:, part], 1, 0).astype(BF16)


def attend_back_kernel(
    column_ref, row_ref, query_ref, key_ref, value_ref, grad_ref, dq_ref, dk_ref, dv_ref
):
    allowed = column_ref[...] == row_ref[...]
    factor = HEAD_SIZE**-0.5
    for start in range(0, LANES, HEAD_SIZE):
        part = slice(start, start + HEAD_SIZE)
        query = query_ref[:, part] * jnp.asarray(factor, BF16)
        key = key_ref[:, part]
        grad = grad_ref[:, part]
        probs = head_probs(query, key, allowed)
        dv_ref[:, part] = dot(probs.astype(BF16), grad, 0, 0).astype(BF16)
        grad_probs = dot(grad, value_ref[:, part], 1, 1)
        weighted = probs * grad_probs
        low = (weighted - probs * jnp.sum(weighted, axis=-1, keepdims=True)).astype(BF16)
        dq_ref[:, part] = (dot(low, key, 1, 0) * factor).astype(BF16)
        dk_ref[:, part] = dot(low, query, 0, 0).astype(BF16)


def attention_call(kernel, outs, labels, mixed, extra):
    micro_count, slot = labels.shape
    rows, width = mixed.shape
    width = width // 3
    groups = width // LANES

    def part(offset):
        return pl.BlockSpec((slot, LANES), lambda b, h: (b, offset + h))

    return pl.pallas_call(
        kernel,
        grid=(micro_count, groups),
        in_specs=[
            pl.BlockSpec((slot, 1), lambda b, h: (b, 0)),
            pl.BlockSpec((None, 1, slot), lambda b, h: (b, 0, 0)),
            part(0),
            part(groups),
            part(2 * groups),
        ]
        + [part(0)] * len(extra),
        out_specs=[part(0)] * outs,
        out_shape=[jax.ShapeDtypeStruct((rows, width), BF16)] * outs,
        compiler_params=pltpu.CompilerParams(vmem_limit_bytes=VMEM_BYTES),
        cost_estimate=pl.CostEstimate(
            flops=rows * slot * width * 4 * (1 + 2 * outs // 3 * 2),
            bytes_accessed=rows * width * 2 * (3 + outs + len(extra)),
            transcendentals=rows * slot * HEADS,
        ),
    )(labels.reshape(rows, 1), labels.reshape(micro_count, 1, slot), mixed, mixed, mixed, *extra)


def up_kernel(hidden_ref, weight_ref, bias_ref, activ_ref, slope_ref):
    pre_act = dot(hidden_ref[...], weight_ref[...], 1, 0) + bias_ref[...]
    cumulative = 0.5 + 0.5 * lax.erf(pre_act * math.sqrt(0.5))
    density = jnp.exp(-0.5 * pre_act * pre_act) * (1.0 / math.sqrt(2.0 * math.pi))
    activ_ref[...] = (pre_act * cumulative).astype(BF16)
    slope_ref[...] = (cumulative + pre_act * density).astype(BF16)


def up_call(hidden_low, weight, bias):
    rows, width = hidden_low.shape
    units = weight.shape[1]
    block = 512
    tall = rows // 2
    return pl.pallas_call(
        up_kernel,
        grid=(units // block, 2),
        in_specs=[
            pl.BlockSpec((tall, width), lambda i, j: (j, 0)),
            pl.BlockSpec((width, block), lambda i, j: (0, i)),
            pl.BlockSpec((1, block), lambda i, j: (0, i)),
        ],
        out_specs=[pl.BlockSpec((tall, block), lambda i, j: (j, i))] * 2,
        out_shape=[jax.ShapeDtypeStruct((rows, units), BF16)] * 2,
        compiler_params=pltpu.CompilerParams(vmem_limit_bytes=VMEM_BYTES),
        cost_estimate=pl.CostEstimate(
            flops=2 * rows * width * units,
            bytes_accessed=2 * (width * units + 2 * rows * units),
            transcendentals=2 * rows * units,
        ),
    )(hidden_low, weight, bias.reshape(1, units))


def halve(blocks, bits_left, bit, device, count, final):
    axis = bits_left.index(bit)
    mine = (device >> bit) & 1
    kept = lax.dynamic_index_in_dim(blocks, mine, axis, keepdims=False)
    sent = lax.dynamic_index_in_dim(blocks, 1 - mine, axis, keepdims=False)
    partners = [(i, i ^ (1 << bit)) for i in range(count)]
    arrived = lax.ppermute(sent, "dp", partners)
    total = kept.astype(F32) + arrived.astype(F32)
    left = [other for other in bits_left if other != bit]
    return (total if final else total.astype(blocks.dtype), left)


def scatter_sum(blocks, orders, device, count):
    levels = count.bit_length() - 1
    columns = blocks.shape[-1]
    tail = blocks.shape[1:]
    left = list(range(levels - 1, -1, -1))
    split = blocks.reshape((2,) * levels + tail)
    split, left = halve(split, left, 0, device, count, levels == 1)
    pieces = []
    width = columns // len(orders)
    for index, order in enumerate(orders):
        part = lax.slice_in_dim(split, index * width, (index + 1) * width, axis=split.ndim - 1)
        rest = left
        for step, bit in enumerate(order):
            part, rest = halve(part, rest, bit, device, count, step == len(order) - 1)
        pieces.append(part)
    return pieces[0] if len(pieces) == 1 else jnp.concatenate(pieces, axis=-1)


def body(
    count,
    inputs,
    seq_lengths,
    qkv_weight,
    out_weight,
    up_weight,
    down_weight,
    query_bias,
    value_bias,
    out_bias,
    up_bias,
    down_bias,
    first_gain,
    first_shift,
    second_gain,
    second_shift,
    grad_output,
):
    device = lax.axis_index("dp")
    levels = count.bit_length() - 1
    high = list(range(1, levels))
    order_one = high
    order_two = high[1:] + high[:1]
    rows, width = inputs.shape
    micro_count = seq_lengths.shape[0]
    slot = rows // micro_count

    small = (
        query_bias,
        value_bias,
        out_bias,
        up_bias,
        down_bias,
        first_gain,
        first_shift,
        second_gain,
        second_shift,
    )
    sizes = [vector.shape[0] for vector in small]
    packed = lax.all_gather(jnp.concatenate(small), "dp", axis=0, tiled=False)
    whole_qkv = lax.all_gather(qkv_weight, "dp", axis=0, tiled=True)
    whole_out = lax.all_gather(out_weight, "dp", axis=0, tiled=True)
    whole_up = lax.all_gather(up_weight, "dp", axis=0, tiled=True)
    whole_down = lax.all_gather(down_weight, "dp", axis=0, tiled=True)
    vectors = []
    start = 0
    for size in sizes:
        vectors.append(packed[:, start : start + size].reshape(-1).astype(F32))
        start += size
    (
        bias_query,
        bias_value,
        bias_out,
        bias_up,
        bias_down,
        gain_first,
        shift_first,
        gain_second,
        shift_second,
    ) = vectors

    seq_ends = jnp.cumsum(seq_lengths, axis=1)
    places = jnp.arange(slot, dtype=jnp.int32)
    labels = jnp.sum((places[None, :, None] >= seq_ends[:, None, :]).astype(jnp.int32), axis=2)

    bias_all = jnp.concatenate([bias_query, jnp.zeros_like(bias_query), bias_value])
    mixed_low = (dot(inputs, whole_qkv, 1, 0) + bias_all).astype(BF16)
    (attended_low,) = attention_call(attend_kernel, 1, labels, mixed_low, ())
    branch = dot(attended_low, whole_out, 1, 0) + bias_out
    hidden, scaled_first, inverse_first = norm_rows(
        inputs.astype(F32) + branch, gain_first, shift_first
    )
    hidden_low = hidden.astype(BF16)
    activ_low, slope_low = up_call(hidden_low, whole_up, bias_up)
    second = dot(activ_low, whole_down, 1, 0) + bias_down
    result, scaled_second, inverse_second = norm_rows(hidden + second, gain_second, shift_second)

    grad_second_in, grad_gain_two, grad_shift_two = norm_back(
        grad_output.astype(F32), scaled_second, inverse_second, gain_second
    )
    grad_branch_two = grad_second_in.astype(BF16)
    grad_down_bias = jnp.sum(grad_branch_two.astype(F32), axis=0)
    grad_down = dot(activ_low, grad_branch_two, 0, 0).astype(BF16)
    grad_down, grad_branch_two = lax.optimization_barrier((grad_down, grad_branch_two))
    sum_down = scatter_sum(
        grad_down.reshape(count, -1, width), (order_one, order_two), device, count
    )

    grad_pre = dot(grad_branch_two, whole_down, 1, 1) * slope_low.astype(F32)
    grad_pre_low = grad_pre.astype(BF16)
    grad_up_bias = jnp.sum(grad_pre_low.astype(F32), axis=0)
    grad_up = dot(hidden_low, grad_pre_low, 0, 0).astype(BF16)
    grad_up, grad_pre_low = lax.optimization_barrier((grad_up, grad_pre_low))
    sum_up = scatter_sum(
        grad_up.reshape(count, -1, grad_up.shape[1]), (order_one, order_two), device, count
    )

    grad_hidden = grad_second_in + dot(grad_pre_low, whole_up, 1, 1)
    grad_first_in, grad_gain_one, grad_shift_one = norm_back(
        grad_hidden, scaled_first, inverse_first, gain_first
    )
    grad_branch_one = grad_first_in.astype(BF16)
    grad_out_bias = jnp.sum(grad_branch_one.astype(F32), axis=0)
    grad_out = dot(attended_low, grad_branch_one, 0, 0).astype(BF16)
    grad_out, grad_branch_one = lax.optimization_barrier((grad_out, grad_branch_one))
    sum_out = scatter_sum(grad_out.reshape(count, -1, width), (order_two,), device, count)

    grad_attended = dot(grad_branch_one, whole_out, 1, 1).astype(BF16)
    grads = attention_call(attend_back_kernel, 3, labels, mixed_low, (grad_attended,))
    grad_mixed = jnp.concatenate(grads, axis=1)
    grad_query_bias = jnp.sum(grads[0].astype(F32), axis=0)
    grad_value_bias = jnp.sum(grads[2].astype(F32), axis=0)
    grad_qkv = dot(inputs, grad_mixed, 0, 0).astype(BF16)
    grad_qkv, grad_mixed = lax.optimization_barrier((grad_qkv, grad_mixed))
    sum_qkv = scatter_sum(
        grad_qkv.reshape(count, -1, 3 * width), (order_one, order_two), device, count
    )
    grad_small = jnp.concatenate(
        [
            vector.reshape(count, -1)
            for vector in (
                grad_query_bias,
                grad_value_bias,
                grad_out_bias,
                grad_up_bias,
                grad_down_bias,
                grad_gain_one,
                grad_shift_one,
                grad_gain_two,
                grad_shift_two,
            )
        ],
        axis=1,
    )
    sum_small = scatter_sum(grad_small[:, None, :], (order_one,), device, count)[0]
    grad_tokens = grad_first_in + dot(grad_mixed, whole_qkv, 1, 1)

    shares = []
    start = 0
    for size in sizes:
        shares.append(sum_small[start : start + size])
        start += size
    return (
        result.astype(BF16),
        grad_tokens.astype(BF16),
        sum_qkv,
        sum_out,
        sum_up,
        sum_down,
        *shares,
    )


def solution(mesh):
    matrix, vector = P("dp", None), P("dp")
    return jax.shard_map(
        functools.partial(body, mesh.shape["dp"]),
        mesh=mesh,
        in_specs=(matrix,) * 6 + (vector,) * 9 + (matrix,),
        out_specs=(matrix,) * 6 + (vector,) * 9,
        check_vma=False,
    )
```

```python
import functools
import math

import jax
import jax.numpy as jnp
from jax import lax
from jax.experimental import pallas as pl
from jax.experimental.pallas import tpu as pltpu
from jax.sharding import PartitionSpec as P

HEADS = 16
HEAD_SIZE = 64
LANES = 128
epsilon = 1e-05
VMEM_BYTES = 48 * 1024 * 1024
F32 = jnp.float32
BF16 = jnp.bfloat16


def dot(left, right, left_dim, right_dim):
    return lax.dot_general(
        left, right, (((left_dim,), (right_dim,)), ((), ())), preferred_element_type=F32
    )


def norm_rows(values, norm_gain, norm_shift):
    center = values - jnp.mean(values, axis=-1, keepdims=True)
    variance = jnp.mean(center * center, axis=-1, keepdims=True)
    inverse = lax.rsqrt(variance + epsilon)
    scaled = center * inverse
    return (scaled * norm_gain + norm_shift, scaled, inverse)


def norm_back(gradient, scaled, inverse, norm_gain):
    weighted = gradient * norm_gain
    mean_grad = jnp.mean(weighted, axis=-1, keepdims=True)
    mean_prod = jnp.mean(weighted * scaled, axis=-1, keepdims=True)
    result = inverse * (weighted - mean_grad - scaled * mean_prod)
    return (result, jnp.sum(gradient * scaled, axis=0), jnp.sum(gradient, axis=0))


def head_probs(query, key, allowed):
    scores = jnp.where(allowed, dot(query, key, 1, 1), -1e30)
    expo = jnp.exp(scores - jnp.max(scores, axis=-1, keepdims=True))
    return expo * (1.0 / jnp.sum(expo, axis=-1, keepdims=True))


def attend_kernel(column_ref, row_ref, query_ref, key_ref, value_ref, out_ref):
    allowed = column_ref[...] == row_ref[...]
    for start in range(0, LANES, HEAD_SIZE):
        part = slice(start, start + HEAD_SIZE)
        query = query_ref[:, part] * jnp.asarray(HEAD_SIZE**-0.5, BF16)
        probs = head_probs(query, key_ref[:, part], allowed)
        out_ref[:, part] = dot(probs.astype(BF16), value_ref[:, part], 1, 0).astype(BF16)


def attend_back_kernel(
    column_ref, row_ref, query_ref, key_ref, value_ref, grad_ref, dq_ref, dk_ref, dv_ref
):
    allowed = column_ref[...] == row_ref[...]
    factor = HEAD_SIZE**-0.5
    for start in range(0, LANES, HEAD_SIZE):
        part = slice(start, start + HEAD_SIZE)
        query = query_ref[:, part] * jnp.asarray(factor, BF16)
        key = key_ref[:, part]
        grad = grad_ref[:, part]
        probs = head_probs(query, key, allowed)
        dv_ref[:, part] = dot(probs.astype(BF16), grad, 0, 0).astype(BF16)
        grad_probs = dot(grad, value_ref[:, part], 1, 1)
        weighted = probs * grad_probs
        low = (weighted - probs * jnp.sum(weighted, axis=-1, keepdims=True)).astype(BF16)
        dq_ref[:, part] = (dot(low, key, 1, 0) * factor).astype(BF16)
        dk_ref[:, part] = dot(low, query, 0, 0).astype(BF16)


def attention_call(kernel, outs, labels, mixed, extra):
    micro_count, slot = labels.shape
    rows, width = mixed.shape
    width = width // 3
    groups = width // LANES

    def part(offset):
        return pl.BlockSpec((slot, LANES), lambda b, h: (b, offset + h))

    return pl.pallas_call(
        kernel,
        grid=(micro_count, groups),
        in_specs=[
            pl.BlockSpec((slot, 1), lambda b, h: (b, 0)),
            pl.BlockSpec((None, 1, slot), lambda b, h: (b, 0, 0)),
            part(0),
            part(groups),
            part(2 * groups),
        ]
        + [part(0)] * len(extra),
        out_specs=[part(0)] * outs,
        out_shape=[jax.ShapeDtypeStruct((rows, width), BF16)] * outs,
        compiler_params=pltpu.CompilerParams(vmem_limit_bytes=VMEM_BYTES),
        cost_estimate=pl.CostEstimate(
            flops=rows * slot * width * 4 * (1 + 2 * outs // 3 * 2),
            bytes_accessed=rows * width * 2 * (3 + outs + len(extra)),
            transcendentals=rows * slot * HEADS,
        ),
    )(labels.reshape(rows, 1), labels.reshape(micro_count, 1, slot), mixed, mixed, mixed, *extra)


def up_kernel(hidden_ref, weight_ref, bias_ref, activ_ref, slope_ref):
    pre_act = dot(hidden_ref[...], weight_ref[...], 1, 0) + bias_ref[...]
    cumulative = 0.5 + 0.5 * lax.erf(pre_act * math.sqrt(0.5))
    density = jnp.exp(-0.5 * pre_act * pre_act) * (1.0 / math.sqrt(2.0 * math.pi))
    activ_ref[...] = (pre_act * cumulative).astype(BF16)
    slope_ref[...] = (cumulative + pre_act * density).astype(BF16)


def up_call(hidden_low, weight, bias):
    rows, width = hidden_low.shape
    units = weight.shape[1]
    block = 512
    tall = rows // 2
    return pl.pallas_call(
        up_kernel,
        grid=(units // block, 2),
        in_specs=[
            pl.BlockSpec((tall, width), lambda i, j: (j, 0)),
            pl.BlockSpec((width, block), lambda i, j: (0, i)),
            pl.BlockSpec((1, block), lambda i, j: (0, i)),
        ],
        out_specs=[pl.BlockSpec((tall, block), lambda i, j: (j, i))] * 2,
        out_shape=[jax.ShapeDtypeStruct((rows, units), BF16)] * 2,
        compiler_params=pltpu.CompilerParams(vmem_limit_bytes=VMEM_BYTES),
        cost_estimate=pl.CostEstimate(
            flops=2 * rows * width * units,
            bytes_accessed=2 * (width * units + 2 * rows * units),
            transcendentals=2 * rows * units,
        ),
    )(hidden_low, weight, bias.reshape(1, units))


def halve(blocks, bits_left, bit, device, count, final):
    axis = bits_left.index(bit)
    mine = (device >> bit) & 1
    kept = lax.dynamic_index_in_dim(blocks, mine, axis, keepdims=False)
    sent = lax.dynamic_index_in_dim(blocks, 1 - mine, axis, keepdims=False)
    partners = [(i, i ^ (1 << bit)) for i in range(count)]
    arrived = lax.ppermute(sent, "dp", partners)
    total = kept.astype(F32) + arrived.astype(F32)
    left = [other for other in bits_left if other != bit]
    return (total if final else total.astype(blocks.dtype), left)


def scatter_sum(blocks, orders, device, count):
    levels = count.bit_length() - 1
    columns = blocks.shape[-1]
    tail = blocks.shape[1:]
    left = list(range(levels - 1, -1, -1))
    split = blocks.reshape((2,) * levels + tail)
    split, left = halve(split, left, 0, device, count, levels == 1)
    pieces = []
    width = columns // len(orders)
    for index, order in enumerate(orders):
        part = lax.slice_in_dim(split, index * width, (index + 1) * width, axis=split.ndim - 1)
        rest = left
        for step, bit in enumerate(order):
            part, rest = halve(part, rest, bit, device, count, step == len(order) - 1)
        pieces.append(part)
    return pieces[0] if len(pieces) == 1 else jnp.concatenate(pieces, axis=-1)


def body(
    count,
    inputs,
    seq_lengths,
    qkv_weight,
    out_weight,
    up_weight,
    down_weight,
    query_bias,
    value_bias,
    out_bias,
    up_bias,
    down_bias,
    first_gain,
    first_shift,
    second_gain,
    second_shift,
    grad_output,
):
    device = lax.axis_index("dp")
    levels = count.bit_length() - 1
    high = list(range(1, levels))
    order_one = high
    order_two = high[1:] + high[:1]
    rows, width = inputs.shape
    micro_count = seq_lengths.shape[0]
    slot = rows // micro_count

    small = (
        query_bias,
        value_bias,
        out_bias,
        up_bias,
        down_bias,
        first_gain,
        first_shift,
        second_gain,
        second_shift,
    )
    sizes = [vector.shape[0] for vector in small]
    packed = lax.all_gather(jnp.concatenate(small), "dp", axis=0, tiled=False)
    whole_qkv = lax.all_gather(qkv_weight, "dp", axis=0, tiled=True)
    whole_out = lax.all_gather(out_weight, "dp", axis=0, tiled=True)
    whole_up = lax.all_gather(up_weight, "dp", axis=0, tiled=True)
    whole_down = lax.all_gather(down_weight, "dp", axis=0, tiled=True)
    vectors = []
    start = 0
    for size in sizes:
        vectors.append(packed[:, start : start + size].reshape(-1).astype(F32))
        start += size
    (
        bias_query,
        bias_value,
        bias_out,
        bias_up,
        bias_down,
        gain_first,
        shift_first,
        gain_second,
        shift_second,
    ) = vectors

    seq_ends = jnp.cumsum(seq_lengths, axis=1)
    places = jnp.arange(slot, dtype=jnp.int32)
    labels = jnp.sum((places[None, :, None] >= seq_ends[:, None, :]).astype(jnp.int32), axis=2)

    bias_all = jnp.concatenate([bias_query, jnp.zeros_like(bias_query), bias_value])
    mixed_low = (dot(inputs, whole_qkv, 1, 0) + bias_all).astype(BF16)
    (attended_low,) = attention_call(attend_kernel, 1, labels, mixed_low, ())
    branch = dot(attended_low, whole_out, 1, 0) + bias_out
    hidden, scaled_first, inverse_first = norm_rows(
        inputs.astype(F32) + branch, gain_first, shift_first
    )
    hidden_low = hidden.astype(BF16)
    activ_low, slope_low = up_call(hidden_low, whole_up, bias_up)
    second = dot(activ_low, whole_down, 1, 0) + bias_down
    result, scaled_second, inverse_second = norm_rows(hidden + second, gain_second, shift_second)

    grad_second_in, grad_gain_two, grad_shift_two = norm_back(
        grad_output.astype(F32), scaled_second, inverse_second, gain_second
    )
    grad_branch_two = grad_second_in.astype(BF16)
    grad_down_bias = jnp.sum(grad_branch_two.astype(F32), axis=0)
    grad_down = dot(activ_low, grad_branch_two, 0, 0).astype(BF16)
    grad_down, grad_branch_two = lax.optimization_barrier((grad_down, grad_branch_two))
    sum_down = scatter_sum(
        grad_down.reshape(count, -1, width), (order_one, order_two), device, count
    )

    grad_pre = dot(grad_branch_two, whole_down, 1, 1) * slope_low.astype(F32)
    grad_pre_low = grad_pre.astype(BF16)
    grad_up_bias = jnp.sum(grad_pre_low.astype(F32), axis=0)
    grad_up = dot(hidden_low, grad_pre_low, 0, 0).astype(BF16)
    grad_up, grad_pre_low = lax.optimization_barrier((grad_up, grad_pre_low))
    sum_up = scatter_sum(
        grad_up.reshape(count, -1, grad_up.shape[1]), (order_one, order_two), device, count
    )

    grad_hidden = grad_second_in + dot(grad_pre_low, whole_up, 1, 1)
    grad_first_in, grad_gain_one, grad_shift_one = norm_back(
        grad_hidden, scaled_first, inverse_first, gain_first
    )
    grad_branch_one = grad_first_in.astype(BF16)
    grad_out_bias = jnp.sum(grad_branch_one.astype(F32), axis=0)
    grad_out = dot(attended_low, grad_branch_one, 0, 0).astype(BF16)
    grad_out, grad_branch_one = lax.optimization_barrier((grad_out, grad_branch_one))
    sum_out = scatter_sum(grad_out.reshape(count, -1, width), (order_two,), device, count)

    grad_attended = dot(grad_branch_one, whole_out, 1, 1).astype(BF16)
    grads = attention_call(attend_back_kernel, 3, labels, mixed_low, (grad_attended,))
    grads, sum_down = lax.optimization_barrier((grads, sum_down))
    grad_mixed = jnp.concatenate(grads, axis=1)
    grad_query_bias = jnp.sum(grads[0].astype(F32), axis=0)
    grad_value_bias = jnp.sum(grads[2].astype(F32), axis=0)
    grad_qkv = dot(inputs, grad_mixed, 0, 0).astype(BF16)
    grad_qkv, grad_mixed = lax.optimization_barrier((grad_qkv, grad_mixed))
    sum_qkv = scatter_sum(
        grad_qkv.reshape(count, -1, 3 * width), (order_one, order_two), device, count
    )
    grad_small = jnp.concatenate(
        [
            vector.reshape(count, -1)
            for vector in (
                grad_query_bias,
                grad_value_bias,
                grad_out_bias,
                grad_up_bias,
                grad_down_bias,
                grad_gain_one,
                grad_shift_one,
                grad_gain_two,
                grad_shift_two,
            )
        ],
        axis=1,
    )
    sum_small = scatter_sum(grad_small[:, None, :], (order_one,), device, count)[0]
    grad_mixed, sum_up = lax.optimization_barrier((grad_mixed, sum_up))
    grad_tokens = grad_first_in + dot(grad_mixed, whole_qkv, 1, 1)

    shares = []
    start = 0
    for size in sizes:
        shares.append(sum_small[start : start + size])
        start += size
    return (
        result.astype(BF16),
        grad_tokens.astype(BF16),
        sum_qkv,
        sum_out,
        sum_up,
        sum_down,
        *shares,
    )


def solution(mesh):
    matrix, vector = P("dp", None), P("dp")
    return jax.shard_map(
        functools.partial(body, mesh.shape["dp"]),
        mesh=mesh,
        in_specs=(matrix,) * 6 + (vector,) * 9 + (matrix,),
        out_specs=(matrix,) * 6 + (vector,) * 9,
        check_vma=False,
    )
```
